1024 devices in a mesh: wide: 32 (over x_hi, y, core), narrow: 32 (over x_lo, z).
Axes of the slice: x: 4 (x_hi: 2, x_lo: 2; x = x_hi * 2 + x_lo), y: 8, z: 16, core: 2. Of those that a mesh axis runs over, the one named last changes fastest.
Arguments:
- points: bfloat16 [262144, 1024], P(('wide', 'narrow')), may hold values from -6 to 6
- centers: bfloat16 [3, 4096, 1024], P(None, 'wide'), may hold values from -6 to 6
- moving: int32 [3, 2048], P(None, ('wide', 'narrow')), may hold values from 0 to 1, as said below
- sent_counts: int32 [3, 1024], P(None, ('wide', 'narrow')), may hold values from 1 to 2, as said below
Outputs:
- new_centers: float32 [3, 4096, 1024], P(None, 'wide')
The draws below stay inside these ranges and needn't reach their ends.
Inputs may be any that keep to these rules, and one draw needn't show every extreme that they name: `moving`: in section s a device's number of entries 1 equals its entry of sent_counts and its partner's count (partner: wide index differing in bit s, same narrow index). `sent_counts`: A device's count equals its partner's in that section; in every section some pair of partners sends exactly 2 blocks each.
All inputs are finite; a program needn't handle non-finite values.
Results may differ from the reference program's by a relative error of at most 0.0055.
Values may be sent and summed in bfloat16 or wider, within the bound.
No kernel may reach another device: no remote copies, remote signals or barrier semaphores. Data moves between devices by JAX's collectives and lax.ppermute only.
A program may use at most 32 MiB of HBM per device.

```python
import jax
import jax.numpy as jnp
from jax import lax

D = 1024
K = 128
BLK = 128
SECTIONS = 3
P_DEV = 256
BLOCKS = 2
CAP = 2
NPTS = 262144
CENTERS = 4096
N_WIDE = 32
N_NARROW = 32
DEVICES = 1024


def move_counts(key):
    grid_key = jax.random.fold_in(key, 41)
    counts_grid = jax.random.randint(grid_key, (SECTIONS, N_WIDE, N_NARROW), 1, CAP + 1)
    wide_index = jnp.arange(N_WIDE, dtype=jnp.int32)
    stacked = []
    for section_num in range(SECTIONS):
        section_key = jax.random.fold_in(grid_key, 100 + section_num)
        chosen_wide = jax.random.randint(section_key, (), 0, N_WIDE)
        chosen_narrow = jax.random.randint(jax.random.fold_in(section_key, 1), (), 0, N_NARROW)
        lowered = chosen_wide - jnp.bitwise_and(chosen_wide, 1 << section_num)
        level_grid = counts_grid[section_num].at[lowered, chosen_narrow].set(CAP)
        paired = wide_index - jnp.bitwise_and(wide_index, 1 << section_num)
        stacked.append(level_grid[paired])
    return jnp.stack(stacked).astype(jnp.int32)


def shuffle_slots(single_key):
    return jax.random.permutation(single_key, BLOCKS)


def draw_sent_counts(key, part):
    counts_grid = move_counts(key)
    return counts_grid.reshape(SECTIONS, DEVICES)


def draw_moving(key, part):
    counts_grid = move_counts(key)
    key = jax.random.fold_in(key, 5)
    all_keys = jax.random.split(key, SECTIONS * DEVICES)
    orders = jax.vmap(shuffle_slots)(all_keys).reshape(SECTIONS, DEVICES, BLOCKS)
    flags = (orders < counts_grid.reshape(SECTIONS, DEVICES, 1)).astype(jnp.int32)
    return flags.reshape(SECTIONS, DEVICES * BLOCKS)


def levels(own_key, dims, shards, smallest, largest):
    gain = 1.0
    for axis_at, blocks in shards:
        draws = jax.random.uniform(jax.random.fold_in(jax.random.fold_in(own_key, 6), axis_at), (blocks,), jnp.float32, smallest / len(shards), largest / len(shards))
        gain = gain * jnp.repeat(jnp.exp(draws), dims[axis_at] // blocks).reshape((-1,) + (1,) * (len(dims) - 1 - axis_at))
    return gain


def noise(stream_key, extent, scale, most, cuts=(), held_as=jnp.bfloat16):
    entries = scale * jax.random.normal(stream_key, extent, jnp.float32)
    if cuts:
        entries = entries * levels(stream_key, extent, cuts, -0.22, 0.18)
    return jnp.clip(entries, -most, most).astype(held_as)


def setup_inputs(seed: int = 0) -> dict:
    seeds = jax.random.split(jax.random.key(seed), 5)
    points = noise(seeds[0], (NPTS, D), 1.0, 6.0, ((0, 1024),))
    centers = noise(seeds[1], (SECTIONS, CENTERS, D), 1.0, 6.0, ((1, 32),))
    moving = draw_moving(jax.random.fold_in(seeds[4], 71), 0)
    sent_counts = draw_sent_counts(jax.random.fold_in(seeds[4], 71), 0)
    return {"points": points, "centers": centers, "moving": moving, "sent_counts": sent_counts}


EPS = 1e-06
SHARPNESS = 80.0

def unit_rows(values):
    widened = values.astype(jnp.float32)
    return widened * lax.rsqrt(lax.optimization_barrier(jnp.mean(widened * widened, axis=-1, keepdims=True)) + EPS)

def slab_update(pair):
    slab_rows, slab_centers = pair
    unit = unit_rows(slab_rows).astype(jnp.bfloat16)
    cunit = unit_rows(slab_centers).astype(jnp.bfloat16)
    scores = jnp.dot(unit, cunit.T, preferred_element_type=jnp.float32) * (SHARPNESS / D)
    raised = jnp.exp(scores)
    weights = (raised / lax.optimization_barrier(jnp.sum(raised, axis=-1, keepdims=True))).astype(jnp.bfloat16)
    sums = jnp.dot(weights.T, unit, preferred_element_type=jnp.float32)
    return unit_rows(sums)

def reference(points, centers, moving, sent_counts):
    layout = points.reshape(N_WIDE, N_NARROW, BLOCKS, BLK * D)
    slot_ids = jnp.arange(CAP, dtype=jnp.int32)
    block_ids = jnp.arange(BLOCKS, dtype=jnp.int32)
    wide_index = jnp.arange(N_WIDE, dtype=jnp.int32)
    outputs = []
    for section_num in range(SECTIONS):
        flags = moving[section_num].reshape(N_WIDE, N_NARROW, BLOCKS).astype(jnp.int32)
        counts = sent_counts[section_num].reshape(N_WIDE, N_NARROW).astype(jnp.int32)
        ranks = (jnp.cumsum(flags, axis=-1) - 1).astype(jnp.int32)
        chosen = (flags == 1) & (ranks < counts[..., None])
        match = chosen[..., None, :] & (ranks[..., None, :] == slot_ids[:, None])
        source = lax.optimization_barrier(jnp.sum(jnp.where(match, block_ids, 0), axis=-1)).astype(jnp.int32)
        valid = jnp.any(match, axis=-1)
        picked = jnp.take_along_axis(layout, source[..., None], axis=2)
        outgoing = jnp.where(valid[..., None], picked, jnp.zeros((), jnp.bfloat16))
        partner = jnp.bitwise_xor(wide_index, 1 << section_num).astype(jnp.int32)
        incoming = outgoing[partner]
        placed = jnp.take_along_axis(incoming, jnp.clip(ranks, 0, CAP - 1)[..., None], axis=2)
        layout = jnp.where(chosen[..., None], placed, layout)
        slab_rows = layout.reshape(N_WIDE, N_NARROW * P_DEV, D)
        slab_centers = centers[section_num].reshape(N_WIDE, K, D)
        updated = lax.map(slab_update, (slab_rows, slab_centers))
        outputs.append(updated.reshape(CENTERS, D))
    return jnp.stack(outputs)
```

```python
import jax
import jax.numpy as jnp
from jax import lax
from jax.sharding import PartitionSpec as P

EPS = 1e-06
SHARPNESS = 80.0
LANES = 128


def partner(value, axis, mask):
    pairs = [(source, source ^ mask) for source in range(lax.axis_size(axis))]
    return lax.ppermute(value, axis, pairs)


def unit_rows(values):
    widened = values.astype(jnp.float32)
    return widened * lax.rsqrt(jnp.mean(widened * widened, axis=-1, keepdims=True) + EPS)


def local_sums(unit, cunit):
    width = unit.shape[1]
    scores = lax.dot_general(
        unit, cunit, (((1,), (1,)), ((), ())), preferred_element_type=jnp.float32
    ) * (SHARPNESS / width)
    raised = jnp.exp(scores)
    weights = (raised / jnp.sum(raised, axis=-1, keepdims=True)).astype(jnp.bfloat16)
    return lax.dot_general(
        weights, unit, (((0,), (0,)), ((), ())), preferred_element_type=jnp.float32
    )


def rings():
    number = lax.axis_size("narrow")
    return [list(range(number // 2)), list(range(number // 2, number))]


def exchange(values):
    return lax.all_to_all(values, "narrow", 0, 0, axis_index_groups=rings(), tiled=True)


def side():
    return lax.axis_index("narrow") // (lax.axis_size("narrow") // 2)


def pair_sums(total):
    half = total.shape[0] // 2
    mine = side()
    kept = lax.dynamic_slice_in_dim(total, mine * half, half)
    sent = lax.dynamic_slice_in_dim(total, (1 - mine) * half, half).astype(jnp.bfloat16)
    taken = partner(sent, "narrow", lax.axis_size("narrow") // 2)
    return kept + taken.astype(jnp.float32)


def to_chunks(rows):
    return rows.reshape(lax.axis_size("narrow") // 2, -1, LANES)


def to_all(chunk):
    return jnp.broadcast_to(chunk[None], (lax.axis_size("narrow") // 2,) + chunk.shape)


def join_pair(mine):
    other = partner(mine, "narrow", lax.axis_size("narrow") // 2)
    is_upper = side() == 1
    lower = jnp.where(is_upper, other, mine)
    upper = jnp.where(is_upper, mine, other)
    return jnp.concatenate([lower, upper], axis=1).astype(jnp.float32)


def norm_chunk(chunk, width):
    rows = chunk.reshape(-1, width // LANES, LANES)
    mean = jnp.mean(rows * rows, axis=(1, 2), keepdims=True)
    return (rows * lax.rsqrt(mean + EPS)).reshape(chunk.shape).astype(jnp.bfloat16)


def chosen_slots(moving, sent_counts):
    flags, counts = moving.T, sent_counts.T
    ranks = jnp.concatenate([flags[:1], flags[:1] + flags[1:]]) - 1
    chosen = ((flags == 1) & (ranks < counts)).astype(jnp.int32)
    chosen = lax.optimization_barrier(chosen)
    return [[chosen[slot, section] == 1 for slot in range(2)] for section in range(chosen.shape[1])]


def on_device(points, centers, moving, sent_counts):
    rows_dev, width = points.shape
    sections, _ = moving.shape
    half = rows_dev // 2
    end = sections - 1
    chosen = chosen_slots(moving, sent_counts)
    unit = unit_rows(points).astype(jnp.bfloat16)
    cunit = unit_rows(centers).astype(jnp.bfloat16)
    far = partner(cunit[end], "wide", 2**end)
    first, second = unit[:half], unit[half:]
    parts = []
    for section in range(end):
        at_first, at_second = chosen[section]
        outgoing = jnp.concatenate([jnp.where(at_first, first, second), second])
        incoming = partner(outgoing, "wide", 2**section)
        lower, upper = incoming[:half], incoming[half:]
        first = jnp.where(at_first, lower, first)
        second = jnp.where(at_second, jnp.where(at_first, upper, lower), second)
        total = local_sums(jnp.concatenate([first, second]), cunit[section])
        parts.append(to_chunks(pair_sums(total).astype(jnp.bfloat16)))
    leaving = chosen[end]
    sums = [
        local_sums(block, jnp.where(leaves, far, cunit[end]))
        for block, leaves in zip((first, second), leaving)
    ]
    stays = sum(jnp.where(leaves, 0.0, part) for leaves, part in zip(leaving, sums))
    leaves = sum(jnp.where(leaves, part, 0.0) for leaves, part in zip(leaving, sums))
    both = jnp.concatenate([stays.reshape(2, half // 2, width), leaves.reshape(2, half // 2, width)], axis=1)
    paired = pair_sums(both.reshape(2 * half, width))
    gone = partner(paired[half // 2 :].astype(jnp.bfloat16), "wide", 2**end)
    paired = paired[: half // 2] + gone.astype(jnp.float32)
    parts.append(to_chunks(paired.astype(jnp.bfloat16)))
    taken = exchange(jnp.concatenate(parts, axis=1))
    summed = jnp.sum(taken.astype(jnp.float32), axis=0)
    chunk = norm_chunk(summed, width)
    taken = exchange(to_all(chunk))
    taken = jnp.moveaxis(taken.reshape(taken.shape[0], sections, -1, LANES), 1, 0)
    return join_pair(taken.reshape(sections, half // 2, width))


def solution(mesh):
    return jax.shard_map(
        on_device,
        mesh=mesh,
        in_specs=(
            P(("wide", "narrow"), None),
            P(None, "wide", None),
            P(None, ("wide", "narrow")),
            P(None, ("wide", "narrow")),
        ),
        out_specs=P(None, "wide", None),
        check_vma=False,
    )
```

```python
import jax
import jax.numpy as jnp
from jax import lax
from jax.sharding import PartitionSpec as P

EPS = 1e-06
SHARPNESS = 80.0
LANES = 128


def partner(value, axis, mask):
    pairs = [(source, source ^ mask) for source in range(lax.axis_size(axis))]
    return lax.ppermute(value, axis, pairs)


def unit_rows(values):
    widened = values.astype(jnp.float32)
    return widened * lax.rsqrt(jnp.mean(widened * widened, axis=-1, keepdims=True) + EPS)


def local_sums(unit, cunit):
    width = unit.shape[1]
    scores = lax.dot_general(
        unit, cunit, (((1,), (1,)), ((), ())), preferred_element_type=jnp.float32
    ) * (SHARPNESS / width)
    raised = jnp.exp(scores)
    weights = (raised / jnp.sum(raised, axis=-1, keepdims=True)).astype(jnp.bfloat16)
    return lax.dot_general(
        weights, unit, (((0,), (0,)), ((), ())), preferred_element_type=jnp.float32
    )


def rings():
    number = lax.axis_size("narrow")
    ring = number // 2
    return [list(range(base + odd, base + ring, 2)) for base in (0, ring) for odd in (0, 1)]


def squares():
    number = lax.axis_size("narrow")
    ring = number // 2
    return [[at, at + 1, at + ring, at + ring + 1] for at in range(0, ring, 2)]


def exchange(values, groups):
    return lax.all_to_all(values, "narrow", 0, 0, axis_index_groups=groups, tiled=True)


def side():
    return lax.axis_index("narrow") // (lax.axis_size("narrow") // 2)


def square_sums(totals):
    parts = [
        total.astype(jnp.bfloat16).reshape(4, total.shape[0] // 4, -1) for total in totals
    ]
    taken = exchange(jnp.concatenate(parts, axis=1), squares())
    return jnp.split(jnp.sum(taken.astype(jnp.float32), axis=0), len(totals))


def to_chunks(rows):
    return rows.astype(jnp.bfloat16).reshape(lax.axis_size("narrow") // 4, -1, LANES)


def to_all(chunk, number):
    return jnp.broadcast_to(chunk[None], (number,) + chunk.shape)


def norm_chunk(chunk, width):
    rows = chunk.reshape(-1, width // LANES, LANES)
    mean = jnp.mean(rows * rows, axis=(1, 2), keepdims=True)
    return (rows * lax.rsqrt(mean + EPS)).reshape(chunk.shape).astype(jnp.bfloat16)


def chosen_slots(moving, sent_counts):
    flags, counts = moving.T, sent_counts.T
    ranks = jnp.concatenate([flags[:1], flags[:1] + flags[1:]]) - 1
    chosen = ((flags == 1) & (ranks < counts)).astype(jnp.int32)
    chosen = lax.optimization_barrier(chosen)
    return [[chosen[slot, section] == 1 for slot in range(2)] for section in range(chosen.shape[1])]


def on_device(points, centers, moving, sent_counts):
    rows_dev, width = points.shape
    sections, _ = moving.shape
    half = rows_dev // 2
    end = sections - 1
    chosen = chosen_slots(moving, sent_counts)
    unit = unit_rows(points).astype(jnp.bfloat16)
    cunit = unit_rows(centers).astype(jnp.bfloat16)
    far = partner(cunit[end], "wide", 2**end)
    first, second = unit[:half], unit[half:]
    for section in range(end):
        at_first, at_second = chosen[section]
        outgoing = jnp.concatenate([jnp.where(at_first, first, second), second])
        incoming = partner(outgoing, "wide", 2**section)
        lower, upper = incoming[:half], incoming[half:]
        first = jnp.where(at_first, lower, first)
        second = jnp.where(at_second, jnp.where(at_first, upper, lower), second)
        total = local_sums(jnp.concatenate([first, second]), cunit[section])
        if section == 0:
            begun = total
        else:
            middle = total
    leaving = chosen[end]
    sums = [
        local_sums(block, jnp.where(goes, far, cunit[end]))
        for block, goes in zip((first, second), leaving)
    ]
    leaves = sum(jnp.where(goes, part, 0.0) for goes, part in zip(leaving, sums))
    stays = sum(jnp.where(goes, 0.0, part) for goes, part in zip(leaving, sums))
    leaves, begun, middle, stays = square_sums([leaves, begun, middle, stays])
    leaves = partner(leaves.astype(jnp.bfloat16), "wide", 2**end)
    last = stays + leaves.astype(jnp.float32)
    parts = [to_chunks(part) for part in (begun, middle, last)]
    taken = exchange(jnp.concatenate(parts, axis=1), rings())
    summed = jnp.sum(taken.astype(jnp.float32), axis=0)
    chunk = norm_chunk(summed, width)
    taken = exchange(to_all(chunk, taken.shape[0]), rings())
    taken = jnp.moveaxis(taken.reshape(taken.shape[0], sections, -1, LANES), 1, 0)
    taken = taken.reshape(sections, half // 4, width)
    taken = exchange(to_all(taken, 4), squares())
    taken = jnp.moveaxis(taken, 0, 1).reshape(sections, half, width)
    return taken.astype(jnp.float32)


def solution(mesh):
    return jax.shard_map(
        on_device,
        mesh=mesh,
        in_specs=(
            P(("wide", "narrow"), None),
            P(None, "wide", None),
            P(None, ("wide", "narrow")),
            P(None, ("wide", "narrow")),
        ),
        out_specs=P(None, "wide", None),
        check_vma=False,
    )
```

```python
import jax
import jax.numpy as jnp
from jax import lax
from jax.experimental import pallas as pl
from jax.experimental.pallas import tpu as pltpu
from jax.sharding import PartitionSpec as P

EPS = 1e-06
SHARPNESS = 80.0
LANES = 128
STEP = 32


def partner(value, axis, mask):
    pairs = [(source, source ^ mask) for source in range(lax.axis_size(axis))]
    return lax.ppermute(value, axis, pairs)


def unit_rows(values):
    widened = values.astype(jnp.float32)
    return widened * lax.rsqrt(jnp.mean(widened * widened, axis=-1, keepdims=True) + EPS)


def local_sums(unit, cunit):
    width = unit.shape[1]
    scores = lax.dot_general(
        unit, cunit, (((1,), (1,)), ((), ())), preferred_element_type=jnp.float32
    ) * (SHARPNESS / width)
    raised = jnp.exp(scores)
    weights = (raised / jnp.sum(raised, axis=-1, keepdims=True)).astype(jnp.bfloat16)
    return lax.dot_general(
        weights, unit, (((0,), (0,)), ((), ())), preferred_element_type=jnp.float32
    )


def rings():
    number = lax.axis_size("narrow")
    ring = number // 2
    return [list(range(base + odd, base + ring, 2)) for base in (0, ring) for odd in (0, 1)]


def squares():
    number = lax.axis_size("narrow")
    ring = number // 2
    return [[at, at + 1, at + ring, at + ring + 1] for at in range(0, ring, 2)]


def exchange(values, groups):
    return lax.all_to_all(values, "narrow", 0, 0, axis_index_groups=groups, tiled=True)


def side():
    return lax.axis_index("narrow") // (lax.axis_size("narrow") // 2)


def square_sums(totals):
    parts = [
        total.astype(jnp.bfloat16).reshape(4, total.shape[0] // 4, -1) for total in totals
    ]
    taken = exchange(jnp.concatenate(parts, axis=1), squares())
    return jnp.split(jnp.sum(taken.astype(jnp.float32), axis=0), len(totals))


def to_chunks(rows):
    return rows.astype(jnp.bfloat16).reshape(lax.axis_size("narrow") // 4, -1, LANES)


def to_all(chunk, number):
    return jnp.broadcast_to(chunk[None], (number,) + chunk.shape)


def norm_chunk(chunk, width):
    rows = chunk.reshape(-1, width // LANES, LANES)
    mean = jnp.mean(rows * rows, axis=(1, 2), keepdims=True)
    return (rows * lax.rsqrt(mean + EPS)).reshape(chunk.shape).astype(jnp.bfloat16)


def enter_kernel(moving, sent_counts, points, centers, unit, outgoing, chosen, cunit):
    half = points.shape[0] // 2
    for section in range(moving.shape[1]):
        rank = -1
        for slot in range(2):
            flag = moving[slot, section]
            rank = rank + flag
            sends = ((flag == 1) & (rank < sent_counts[0, section])).astype(jnp.int32)
            row = pl.ds(2 * section + slot, 1)
            chosen[row] = jnp.full((1, LANES), sends, jnp.int32)
    at_first = (moving[0, 0] == 1) & (moving[0, 0] - 1 < sent_counts[0, 0])
    start = pl.multiple_of(jnp.where(at_first, 0, half), STEP)

    @pl.loop(0, points.shape[0] // STEP, unroll=True)
    def _(at):
        rows = pl.ds(at * STEP, STEP)
        unit[rows] = unit_rows(points[rows]).astype(jnp.bfloat16)

    @pl.loop(0, half // STEP, unroll=True)
    def _(at):
        outgoing[pl.ds(at * STEP, STEP)] = unit[pl.ds(start + at * STEP, STEP)]
        rows = pl.ds(half + at * STEP, STEP)
        outgoing[rows] = unit[rows]

    for section in range(centers.shape[0]):

        @pl.loop(0, centers.shape[1] // STEP, unroll=True)
        def _(at):
            rows = pl.ds(at * STEP, STEP)
            cunit[section, rows] = unit_rows(centers[section, rows]).astype(jnp.bfloat16)


def enter(points, centers, moving, sent_counts):
    return pl.pallas_call(
        enter_kernel,
        out_shape=(
            pltpu.VMEM(points.shape, jnp.bfloat16),
            pltpu.VMEM(points.shape, jnp.bfloat16),
            pltpu.VMEM((8, LANES), jnp.int32),
            pltpu.VMEM(centers.shape, jnp.bfloat16),
        ),
        in_specs=[
            pl.BlockSpec(memory_space=pltpu.SMEM),
            pl.BlockSpec(memory_space=pltpu.SMEM),
            pl.BlockSpec(memory_space=pltpu.VMEM),
            pl.BlockSpec(memory_space=pltpu.VMEM),
        ],
        out_specs=(pl.BlockSpec(memory_space=pltpu.VMEM),) * 4,
        name="enter",
    )(moving.T, sent_counts.T, points, centers)


def on_device(points, centers, moving, sent_counts):
    rows_dev, width = points.shape
    sections, _ = moving.shape
    half = rows_dev // 2
    end = sections - 1
    unit, sent, flags, cunit = enter(points, centers, moving, sent_counts)
    chosen = [
        [flags[2 * section + slot, 0] == 1 for slot in range(2)] for section in range(sections)
    ]
    far = partner(cunit[end], "wide", 2**end)
    first, second = unit[:half], unit[half:]
    for section in range(end):
        at_first, at_second = chosen[section]
        if section > 0:
            sent = jnp.concatenate([jnp.where(at_first, first, second), second])
        incoming = partner(sent, "wide", 2**section)
        lower, upper = incoming[:half], incoming[half:]
        first = jnp.where(at_first, lower, first)
        second = jnp.where(at_second, jnp.where(at_first, upper, lower), second)
        total = local_sums(jnp.concatenate([first, second]), cunit[section])
        if section == 0:
            begun = total
        else:
            middle = total
    leaving = chosen[end]
    sums = [
        local_sums(block, jnp.where(goes, far, cunit[end]))
        for block, goes in zip((first, second), leaving)
    ]
    leaves = sum(jnp.where(goes, part, 0.0) for goes, part in zip(leaving, sums))
    stays = sum(jnp.where(goes, 0.0, part) for goes, part in zip(leaving, sums))
    leaves, begun, middle, stays = square_sums([leaves, begun, middle, stays])
    leaves = partner(leaves.astype(jnp.bfloat16), "wide", 2**end)
    last = stays + leaves.astype(jnp.float32)
    parts = [to_chunks(part) for part in (begun, middle, last)]
    taken = exchange(jnp.concatenate(parts, axis=1), rings())
    summed = jnp.sum(taken.astype(jnp.float32), axis=0)
    chunk = norm_chunk(summed, width)
    taken = exchange(to_all(chunk, taken.shape[0]), rings())
    taken = jnp.moveaxis(taken.reshape(taken.shape[0], sections, -1, LANES), 1, 0)
    taken = taken.reshape(sections, half // 4, width)
    taken = exchange(to_all(taken, 4), squares())
    taken = jnp.moveaxis(taken, 0, 1).reshape(sections, half, width)
    return taken.astype(jnp.float32)


def solution(mesh):
    return jax.shard_map(
        on_device,
        mesh=mesh,
        in_specs=(
            P(("wide", "narrow"), None),
            P(None, "wide", None),
            P(None, ("wide", "narrow")),
            P(None, ("wide", "narrow")),
        ),
        out_specs=P(None, "wide", None),
        check_vma=False,
    )
```

```python
import jax
import jax.numpy as jnp
from jax import lax
from jax.experimental import pallas as pl
from jax.experimental.pallas import tpu as pltpu
from jax.sharding import PartitionSpec as P

EPS = 1e-06
SHARPNESS = 80.0
LANES = 128
STEP = 32


def partner(value, axis, mask):
    pairs = [(source, source ^ mask) for source in range(lax.axis_size(axis))]
    return lax.ppermute(value, axis, pairs)


def unit_rows(values):
    widened = values.astype(jnp.float32)
    return widened * lax.rsqrt(jnp.mean(widened * widened, axis=-1, keepdims=True) + EPS)


def local_sums(unit, cunit):
    width = unit.shape[1]
    scores = lax.dot_general(
        unit, cunit, (((1,), (1,)), ((), ())), preferred_element_type=jnp.float32
    ) * (SHARPNESS / width)
    raised = jnp.exp(scores)
    weights = (raised / jnp.sum(raised, axis=-1, keepdims=True)).astype(jnp.bfloat16)
    return lax.dot_general(
        weights, unit, (((0,), (0,)), ((), ())), preferred_element_type=jnp.float32
    )


def rings():
    number = lax.axis_size("narrow")
    ring = number // 2
    return [list(range(base + odd, base + ring, 2)) for base in (0, ring) for odd in (0, 1)]


def squares():
    number = lax.axis_size("narrow")
    ring = number // 2
    return [[at, at + 1, at + ring, at + ring + 1] for at in range(0, ring, 2)]


def exchange(values, groups):
    return lax.all_to_all(values, "narrow", 0, 0, axis_index_groups=groups, tiled=True)


def side():
    return lax.axis_index("narrow") // (lax.axis_size("narrow") // 2)


def square_sums(totals):
    parts = [
        total.astype(jnp.bfloat16).reshape(4, total.shape[0] // 4, -1) for total in totals
    ]
    taken = exchange(jnp.concatenate(parts, axis=1), squares())
    return jnp.split(jnp.sum(taken.astype(jnp.float32), axis=0), len(totals))


def to_chunks(rows):
    return rows.astype(jnp.bfloat16).reshape(lax.axis_size("narrow") // 4, -1, LANES)


def to_all(chunk, number):
    return jnp.broadcast_to(chunk[None], (number,) + chunk.shape)


def norm_chunk(chunk, width):
    rows = chunk.reshape(-1, width // LANES, LANES)
    mean = jnp.mean(rows * rows, axis=(1, 2), keepdims=True)
    return (rows * lax.rsqrt(mean + EPS)).reshape(chunk.shape).astype(jnp.bfloat16)


def enter_kernel(moving, sent_counts, points, centers, unit, outgoing, chosen, cunit):
    half = points.shape[0] // 2
    for section in range(moving.shape[1]):
        rank = -1
        for slot in range(2):
            flag = moving[slot, section]
            rank = rank + flag
            sends = ((flag == 1) & (rank < sent_counts[0, section])).astype(jnp.int32)
            row = pl.ds(2 * section + slot, 1)
            chosen[row] = jnp.full((1, LANES), sends, jnp.int32)
    at_first = (moving[0, 0] == 1) & (moving[0, 0] - 1 < sent_counts[0, 0])
    start = pl.multiple_of(jnp.where(at_first, 0, half), STEP)

    @pl.loop(0, points.shape[0] // STEP, unroll=True)
    def _(at):
        rows = pl.ds(at * STEP, STEP)
        unit[rows] = unit_rows(points[rows]).astype(jnp.bfloat16)

    @pl.loop(0, half // STEP, unroll=True)
    def _(at):
        outgoing[pl.ds(at * STEP, STEP)] = unit[pl.ds(start + at * STEP, STEP)]
        rows = pl.ds(half + at * STEP, STEP)
        outgoing[rows] = unit[rows]

    for section in range(centers.shape[0]):

        @pl.loop(0, centers.shape[1] // STEP, unroll=True)
        def _(at):
            rows = pl.ds(at * STEP, STEP)
            cunit[section, rows] = unit_rows(centers[section, rows]).astype(jnp.bfloat16)


def enter(points, centers, moving, sent_counts):
    return pl.pallas_call(
        enter_kernel,
        out_shape=(
            pltpu.VMEM(points.shape, jnp.bfloat16),
            pltpu.VMEM(points.shape, jnp.bfloat16),
            pltpu.VMEM((8, LANES), jnp.int32),
            pltpu.VMEM(centers.shape, jnp.bfloat16),
        ),
        in_specs=[
            pl.BlockSpec(memory_space=pltpu.SMEM),
            pl.BlockSpec(memory_space=pltpu.SMEM),
            pl.BlockSpec(memory_space=pltpu.VMEM),
            pl.BlockSpec(memory_space=pltpu.VMEM),
        ],
        out_specs=(pl.BlockSpec(memory_space=pltpu.VMEM),) * 4,
        name="enter",
    )(moving.T, sent_counts.T, points, centers)


def hold_kernel(values, _, held):
    held[...] = values[...]


def hold(values, earlier):
    return pl.pallas_call(
        hold_kernel,
        out_shape=pltpu.VMEM(values.shape, values.dtype),
        in_specs=[pl.BlockSpec(memory_space=pltpu.VMEM)] * 2,
        out_specs=pl.BlockSpec(memory_space=pltpu.VMEM),
        name="hold",
    )(values, earlier)


def on_device(points, centers, moving, sent_counts):
    rows_dev, width = points.shape
    sections, _ = moving.shape
    half = rows_dev // 2
    end = sections - 1
    unit, sent, flags, cunit = enter(points, centers, moving, sent_counts)
    chosen = [
        [flags[2 * section + slot, 0] == 1 for slot in range(2)] for section in range(sections)
    ]
    far = partner(cunit[end], "wide", 2**end)
    first, second = unit[:half], unit[half:]
    for section in range(end):
        at_first, at_second = chosen[section]
        if section > 0:
            sent = jnp.concatenate([jnp.where(at_first, first, second), second])
        incoming = partner(sent, "wide", 2**section)
        lower, upper = incoming[:half], incoming[half:]
        first = jnp.where(at_first, lower, first)
        second = jnp.where(at_second, jnp.where(at_first, upper, lower), second)
        total = local_sums(jnp.concatenate([first, second]), cunit[section])
        if section == 0:
            (begun,) = square_sums([total])
        else:
            middle = total
    held = hold(flags, begun)
    leaving = [held[2 * end + slot, 0] == 1 for slot in range(2)]
    sums = [
        local_sums(block, jnp.where(goes, far, cunit[end]))
        for block, goes in zip((first, second), leaving)
    ]
    leaves = sum(jnp.where(goes, part, 0.0) for goes, part in zip(leaving, sums))
    stays = sum(jnp.where(goes, 0.0, part) for goes, part in zip(leaving, sums))
    leaves, middle, stays = square_sums([leaves, middle, stays])
    leaves = partner(leaves.astype(jnp.bfloat16), "wide", 2**end)
    last = stays + leaves.astype(jnp.float32)
    parts = [to_chunks(part) for part in (begun, middle, last)]
    taken = exchange(jnp.concatenate(parts, axis=1), rings())
    summed = jnp.sum(taken.astype(jnp.float32), axis=0)
    chunk = norm_chunk(summed, width)
    taken = exchange(to_all(chunk, taken.shape[0]), rings())
    taken = jnp.moveaxis(taken.reshape(taken.shape[0], sections, -1, LANES), 1, 0)
    taken = taken.reshape(sections, half // 4, width)
    taken = exchange(to_all(taken, 4), squares())
    taken = jnp.moveaxis(taken, 0, 1).reshape(sections, half, width)
    return taken.astype(jnp.float32)


def solution(mesh):
    return jax.shard_map(
        on_device,
        mesh=mesh,
        in_specs=(
            P(("wide", "narrow"), None),
            P(None, "wide", None),
            P(None, ("wide", "narrow")),
            P(None, ("wide", "narrow")),
        ),
        out_specs=P(None, "wide", None),
        check_vma=False,
    )
```

```python
import jax
import jax.numpy as jnp
from jax import lax
from jax.experimental import pallas as pl
from jax.experimental.pallas import tpu as pltpu
from jax.sharding import PartitionSpec as P

EPS = 1e-06
SHARPNESS = 80.0
LANES = 128
STEP = 32


def partner(value, axis, mask):
    pairs = [(source, source ^ mask) for source in range(lax.axis_size(axis))]
    return lax.ppermute(value, axis, pairs)


def unit_rows(values):
    widened = values.astype(jnp.float32)
    return widened * lax.rsqrt(jnp.mean(widened * widened, axis=-1, keepdims=True) + EPS)


def local_sums(unit, cunit):
    width = unit.shape[1]
    scores = lax.dot_general(
        unit, cunit, (((1,), (1,)), ((), ())), preferred_element_type=jnp.float32
    ) * (SHARPNESS / width)
    raised = jnp.exp(scores)
    weights = (raised / jnp.sum(raised, axis=-1, keepdims=True)).astype(jnp.bfloat16)
    return lax.dot_general(
        weights, unit, (((0,), (0,)), ((), ())), preferred_element_type=jnp.float32
    )


def rings():
    number = lax.axis_size("narrow")
    ring = number // 2
    return [list(range(base + odd, base + ring, 2)) for base in (0, ring) for odd in (0, 1)]


def squares():
    number = lax.axis_size("narrow")
    ring = number // 2
    return [[at, at + 1, at + ring, at + ring + 1] for at in range(0, ring, 2)]


def exchange(values, groups):
    return lax.all_to_all(values, "narrow", 0, 0, axis_index_groups=groups, tiled=True)


def side():
    return lax.axis_index("narrow") // (lax.axis_size("narrow") // 2)


def square_sums(totals):
    parts = [
        total.astype(jnp.bfloat16).reshape(4, total.shape[0] // 4, -1) for total in totals
    ]
    taken = exchange(jnp.concatenate(parts, axis=1), squares())
    return jnp.split(jnp.sum(taken.astype(jnp.float32), axis=0), len(totals))


def to_chunks(rows):
    return rows.astype(jnp.bfloat16).reshape(lax.axis_size("narrow") // 4, -1, LANES)


def to_all(chunk, number):
    return jnp.broadcast_to(chunk[None], (number,) + chunk.shape)


def norm_chunk(chunk, width):
    rows = chunk.reshape(-1, width // LANES, LANES)
    mean = jnp.mean(rows * rows, axis=(1, 2), keepdims=True)
    return (rows * lax.rsqrt(mean + EPS)).reshape(chunk.shape).astype(jnp.bfloat16)


def enter_kernel(moving, sent_counts, points, centers, unit, outgoing, chosen, cunit):
    half = points.shape[0] // 2
    for section in range(moving.shape[1]):
        rank = -1
        for slot in range(2):
            flag = moving[slot, section]
            rank = rank + flag
            sends = ((flag == 1) & (rank < sent_counts[0, section])).astype(jnp.int32)
            row = pl.ds(2 * section + slot, 1)
            chosen[row] = jnp.full((1, LANES), sends, jnp.int32)
    at_first = (moving[0, 0] == 1) & (moving[0, 0] - 1 < sent_counts[0, 0])
    start = pl.multiple_of(jnp.where(at_first, 0, half), STEP)

    @pl.loop(0, points.shape[0] // STEP, unroll=True)
    def _(at):
        rows = pl.ds(at * STEP, STEP)
        unit[rows] = unit_rows(points[rows]).astype(jnp.bfloat16)

    @pl.loop(0, half // STEP, unroll=True)
    def _(at):
        outgoing[pl.ds(at * STEP, STEP)] = unit[pl.ds(start + at * STEP, STEP)]
        rows = pl.ds(half + at * STEP, STEP)
        outgoing[rows] = unit[rows]

    for section in range(centers.shape[0]):

        @pl.loop(0, centers.shape[1] // STEP, unroll=True)
        def _(at):
            rows = pl.ds(at * STEP, STEP)
            cunit[section, rows] = unit_rows(centers[section, rows]).astype(jnp.bfloat16)


def enter(points, centers, moving, sent_counts):
    return pl.pallas_call(
        enter_kernel,
        out_shape=(
            pltpu.VMEM(points.shape, jnp.bfloat16),
            pltpu.VMEM(points.shape, jnp.bfloat16),
            pltpu.VMEM((8, LANES), jnp.int32),
            pltpu.VMEM(centers.shape, jnp.bfloat16),
        ),
        in_specs=[
            pl.BlockSpec(memory_space=pltpu.SMEM),
            pl.BlockSpec(memory_space=pltpu.SMEM),
            pl.BlockSpec(memory_space=pltpu.VMEM),
            pl.BlockSpec(memory_space=pltpu.VMEM),
        ],
        out_specs=(pl.BlockSpec(memory_space=pltpu.VMEM),) * 4,
        name="enter",
    )(moving.T, sent_counts.T, points, centers)


def hold_kernel(values, _, held):
    held[...] = values[...]


def hold(values, earlier):
    return pl.pallas_call(
        hold_kernel,
        out_shape=pltpu.VMEM(values.shape, values.dtype),
        in_specs=[pl.BlockSpec(memory_space=pltpu.VMEM)] * 2,
        out_specs=pl.BlockSpec(memory_space=pltpu.VMEM),
        name="hold",
    )(values, earlier)


def on_device(points, centers, moving, sent_counts):
    rows_dev, width = points.shape
    sections, _ = moving.shape
    half = rows_dev // 2
    end = sections - 1
    unit, sent, flags, cunit = enter(points, centers, moving, sent_counts)
    chosen = [
        [flags[2 * section + slot, 0] == 1 for slot in range(2)] for section in range(sections)
    ]
    far = partner(cunit[end], "wide", 2**end)
    first, second = unit[:half], unit[half:]
    for section in range(end):
        at_first, at_second = chosen[section]
        if section > 0:
            sent = jnp.concatenate([jnp.where(at_first, first, second), second])
        incoming = partner(sent, "wide", 2**section)
        lower, upper = incoming[:half], incoming[half:]
        first = jnp.where(at_first, lower, first)
        second = jnp.where(at_second, jnp.where(at_first, upper, lower), second)
        total = local_sums(jnp.concatenate([first, second]), cunit[section])
        if section == 0:
            (begun,) = square_sums([total])
        else:
            middle = total
    held = hold(flags, begun[:8, :LANES])
    leaving = [held[2 * end + slot, 0] == 1 for slot in range(2)]
    sums = [
        local_sums(block, jnp.where(goes, far, cunit[end]))
        for block, goes in zip((first, second), leaving)
    ]
    leaves = sum(jnp.where(goes, part, 0.0) for goes, part in zip(leaving, sums))
    stays = sum(jnp.where(goes, 0.0, part) for goes, part in zip(leaving, sums))
    leaves, middle, stays = square_sums([leaves, middle, stays])
    leaves = partner(leaves.astype(jnp.bfloat16), "wide", 2**end)
    last = stays + leaves.astype(jnp.float32)
    parts = [to_chunks(part) for part in (begun, middle, last)]
    taken = exchange(jnp.concatenate(parts, axis=1), rings())
    summed = jnp.sum(taken.astype(jnp.float32), axis=0)
    chunk = norm_chunk(summed, width)
    taken = exchange(to_all(chunk, taken.shape[0]), rings())
    taken = jnp.moveaxis(taken.reshape(taken.shape[0], sections, -1, LANES), 1, 0)
    taken = taken.reshape(sections, half // 4, width)
    taken = exchange(to_all(taken, 4), squares())
    taken = jnp.moveaxis(taken, 0, 1).reshape(sections, half, width)
    return taken.astype(jnp.float32)


def solution(mesh):
    return jax.shard_map(
        on_device,
        mesh=mesh,
        in_specs=(
            P(("wide", "narrow"), None),
            P(None, "wide", None),
            P(None, ("wide", "narrow")),
            P(None, ("wide", "narrow")),
        ),
        out_specs=P(None, "wide", None),
        check_vma=False,
    )
```
